32 devices in a mesh: blk: 32 (over z, y, x, core), mp: 1.
Axes of the slice: x: 2, y: 2, z: 4, core: 2. Of those that a mesh axis runs over, the one named last changes fastest.
Arguments:
- tokens: bfloat16 [8192, 2048], P('blk'), may hold values from -6 to 6
- attn_gain: float32 [2048], replicated, may hold values from 0.1 to 1.9
- w_qkv: bfloat16 [2048, 3, 2048], P(None, None, 'mp'), may hold values from -4 to 4
- w_o: bfloat16 [2048, 2048], P('mp'), may hold values from -2.5 to 2.5
- moe_gain: float32 [2048], replicated, may hold values from 0.1 to 1.9
- w_gate_up: bfloat16 [64, 2048, 2, 1408], P('blk', None, None, 'mp'), may hold values from -0.125 to 0.125
- w_down: bfloat16 [64, 1408, 2048], P('blk', 'mp'), may hold values from -0.15625 to 0.15625
- expert_ids: int32 [8192, 6], P(('blk', 'mp')), may hold values from 0 to 63, all different within a row; in each aligned block of 256 rows (0 to 255, 256 to 511, ...) at most 40 rows name the same one
- gate_weights: bfloat16 [8192, 6], P(('blk', 'mp')), may hold values from 0.049804688 to 0.5
- prompt_lengths: int32 [4], replicated, may hold values from 1 to 4096, 8192 in all
- page_table: int32 [64], P('blk'), may hold values from 0 to 63, each once
Outputs:
- mixed: bfloat16 [8192, 2048], P(('blk', 'mp'))
- kv_cache: bfloat16 [64, 2, 128, 2048], P('blk', None, None, 'mp')
The draws below stay inside these ranges and needn't reach their ends.
Inputs may be any that keep to these rules, and one draw needn't show every extreme that they name: `expert_ids`: each row names 6 different experts; within the rows of one device (aligned blocks of 256 rows) no expert is named by more than 40 rows, a bound that some block reaches. `prompt_lengths`: the lengths sum to 8192; the longest is exactly 4096. `page_table`: each page number appears once.
All inputs are finite; a program needn't handle non-finite values.
Results may differ from the reference program's by a relative error of at most 0.017.
Values may be sent and summed in bfloat16 or wider, within the bound.
No kernel may reach another device: no remote copies, remote signals or barrier semaphores. Data moves between devices by JAX's collectives and lax.ppermute only.
A program may use at most 320 MiB of HBM per device.

```python
import math
import jax
import jax.numpy as jnp
import numpy as np
from jax import lax

D = 2048
HEADS = 16
HD = 128
FF = 1408
TOP = 6
PAGE = 128
TENANTS = 4
TOK_DEV = 256
EXPERTS = 64
TOKENS = 8192
PAGES = 64
CAP = 40
N_BLK = 32
N_MP = 1


def draw_w_qkv(key, part):
    first = jax.random.fold_in(key, 0)
    base = jax.random.normal(first, (D, 3, HEADS * HD), jnp.float32) * D ** (-0.5)
    return jnp.clip(base, -4.0, 4.0).astype(jnp.bfloat16)


def levels(rng, shape, cuts, low, top_value):
    loudness = 1.0
    for dim, shards_of in cuts:
        heights = jax.random.uniform(jax.random.fold_in(jax.random.fold_in(rng, 6), dim), (shards_of,), jnp.float32, low / len(cuts), top_value / len(cuts))
        loudness = loudness * jnp.repeat(jnp.exp(heights), shape[dim] // shards_of).reshape((-1,) + (1,) * (len(shape) - 1 - dim))
    return loudness


def profile(count, total, most, slope):
    loads = [(1 << 20) // math.isqrt(grade ** slope) + 1 for grade in range(2, count + 1)]
    spare, given = total - most - (count - 1), [1] * (count - 1)
    while spare > 0:
        free = [i for i in range(count - 1) if given[i] < most]
        mass, remaining = sum([loads[i] for i in free]), spare
        for i in free:
            more = min(most - given[i], max(1, remaining * loads[i] // mass), spare)
            given[i] = given[i] + more
            spare = spare - more
    return np.array([most] + given)


def ragged_sizes(rng, count, total, limit, slope):
    if count == 2:
        one = jax.random.randint(rng, (), max(1, total - limit), min(limit, total - 1) + 1)
        return jnp.stack([one, total - one])
    sizes = jnp.asarray(profile(count, total, limit, slope), jnp.int32)
    pairs = (count - 1) // 2
    source_of, receiver = sizes[1:1 + 2 * pairs:2], sizes[2:2 + 2 * pairs:2]
    room = jnp.minimum(source_of - 1, limit - receiver)
    shifted = jax.random.randint(jax.random.fold_in(rng, 1), (pairs,), 0, 1 << 20) % (room + 1)
    sizes = sizes.at[1:1 + 2 * pairs:2].set(source_of - shifted).at[2:2 + 2 * pairs:2].set(receiver + shifted)
    return sizes[jax.random.permutation(jax.random.fold_in(rng, 2), count)]


def shared_out(stream_key, own, number, rows, count, top, most, slope):
    ranking = jax.random.permutation(stream_key, count)
    packed, common = shares(count, rows * top, most, slope, True), shares(count, rows * top, most, slope, False)
    places = jnp.arange(count)

    def named(sizes, offset_by):
        used = int((sizes > 0).sum())
        fixed = max(1, used // 4)
        shifted = fixed + (places - fixed + offset_by * (used - fixed)) % max(1, count - fixed)
        return jnp.zeros((count,), jnp.int32).at[ranking[jnp.where(places < fixed, places, shifted)]].set(jnp.asarray(sizes, jnp.int32))

    sizes = jnp.where(number % 4 == 0, named(packed, number // 4), named(common, number - number // 4 - 1))
    mixed = jax.random.permutation(jax.random.fold_in(own, 3), count)
    source_of, taker = mixed[0:count // 2 * 2:2], mixed[1:count // 2 * 2:2]
    margin = jnp.minimum(sizes[source_of] - 1, most - sizes[taker]) // 2
    margin = jnp.where((source_of == ranking[0]) | (taker == ranking[0]) | (sizes[taker] == 0), 0, jnp.maximum(margin, 0))
    shifted = jax.random.randint(jax.random.fold_in(own, 4), (count // 2,), 0, 1 << 20) % (margin + 1)
    sizes = sizes.at[source_of].add(-shifted).at[taker].add(shifted)
    members = jnp.searchsorted(jnp.cumsum(sizes), jnp.arange(rows * top), side="right").astype(jnp.int32)
    table = members.reshape(top, rows).T
    table = table[jax.random.permutation(jax.random.fold_in(own, 1), rows)]
    offset_by = jax.random.randint(jax.random.fold_in(own, 2), (rows, 1), 0, top)
    return jnp.take_along_axis(table, (jnp.arange(top)[None, :] + offset_by) % top, axis=1)


def shares(count, total, bound, skew, full):
    portions = [(1 << 20) // math.isqrt(grade ** skew) + 1 for grade in range(1, count + 1)]
    largest = bound if full else min(bound, max(-(-total // count), total * portions[0] // sum(portions)))
    least = 1 if total - largest >= count - 1 else 0
    holding, rest = [largest] + [least] * (count - 1), total - largest - least * (count - 1)
    while rest > 0:
        free = [i for i in range(1, count) if holding[i] < largest] or [i for i in range(1, count) if holding[i] < bound]
        mass, budget = sum([portions[i] for i in free]), rest
        for i in free:
            addition = min(bound - holding[i], max(1, budget * portions[i] // mass), rest)
            holding[i] = holding[i] + addition
            rest = rest - addition
    return np.array(holding)


def scatter_about(key, dims, spread, bound, pieces=(), kind=jnp.bfloat16):
    result = spread * jax.random.normal(key, dims, jnp.float32)
    if pieces:
        result = result * levels(key, dims, pieces, -0.22, 0.18)
    return jnp.clip(result, -bound, bound).astype(kind)


def setup_inputs(seed: int = 0) -> dict:
    arg_keys = jax.random.split(jax.random.key(seed), 12)
    tokens = scatter_about(arg_keys[0], (TOKENS, D), 1.0, 6.0, ((0, 32),))
    attn_gain = jnp.clip(1.0 + 0.18 * jax.random.normal(arg_keys[1], (D,), jnp.float32), 0.1, 1.9)
    w_qkv = draw_w_qkv(jax.random.fold_in(arg_keys[11], 71), 0)
    w_o = scatter_about(arg_keys[3], (HEADS * HD, D), 0.25, 2.5)
    moe_gain = jnp.clip(1.0 + 0.18 * jax.random.normal(arg_keys[4], (D,), jnp.float32), 0.1, 1.9)
    w_gate_up = scatter_about(arg_keys[5], (EXPERTS, D, 2, FF), D ** -0.5, 0.125, ((0, 32),))
    w_down = scatter_about(arg_keys[6], (EXPERTS, FF, D), FF ** -0.5, 0.15625, ((0, 32),))
    expert_ids_keys = jax.random.split(jax.random.fold_in(arg_keys[7], 1), TOKENS // (TOK_DEV // N_MP))
    expert_ids_turns = jax.random.permutation(jax.random.fold_in(arg_keys[7], 3), TOKENS // (TOK_DEV // N_MP))
    expert_ids = jax.vmap(lambda own, number: shared_out(jax.random.fold_in(arg_keys[7], 2), own, number, TOK_DEV // N_MP, EXPERTS, TOP, CAP, 2))(expert_ids_keys, expert_ids_turns).reshape((TOKENS, TOP))
    gate_weights = jnp.clip(jnp.exp(math.log(0.5) - 2.306499 * jax.random.uniform(arg_keys[8], (TOKENS, TOP), jnp.float32) ** levels(arg_keys[8], (TOKENS, TOP), ((0, 32),), -0.2, 0.2)), 0.049804688, 0.5).astype(jnp.bfloat16)
    prompt_lengths = ragged_sizes(arg_keys[9], TENANTS, TOKENS, TOKENS // 2, 2).astype(jnp.int32)
    page_table = jax.random.permutation(arg_keys[10], PAGES).astype(jnp.int32)
    return dict(tokens=tokens, attn_gain=attn_gain, w_qkv=w_qkv, w_o=w_o, moe_gain=moe_gain, w_gate_up=w_gate_up, w_down=w_down, expert_ids=expert_ids, gate_weights=gate_weights, prompt_lengths=prompt_lengths, page_table=page_table)


EPS = 1e-06
THETA = 10000.0
NEG = -1e+30

def rms_scale(values, gain):
    mean_sq = lax.optimization_barrier(jnp.mean(values * values, axis=-1, keepdims=True))
    return values * lax.rsqrt(mean_sq + EPS) * gain

def rotate(values, relative):
    halfd = values.shape[-1] // 2
    inverse = THETA ** (-jnp.arange(halfd, dtype=jnp.float32) / halfd)
    angle = relative.astype(jnp.float32)[:, None] * inverse[None, :]
    cosine = jnp.cos(angle)[:, None, :]
    sine = jnp.sin(angle)[:, None, :]
    first = values[..., :halfd]
    second = values[..., halfd:]
    return jnp.concatenate([first * cosine - second * sine, second * cosine + first * sine], axis=-1)

def row_positions(rows):
    half = TOK_DEV // 2
    device = rows // TOK_DEV
    inner = rows % TOK_DEV
    return jnp.where(inner < half, device * half + inner, (2 * N_BLK - 1 - device) * half + inner - half).astype(jnp.int32)

def position_rows(positions):
    half = TOK_DEV // 2
    block = positions // half
    inner = positions % half
    return jnp.where(block < N_BLK, block * TOK_DEV + inner, (2 * N_BLK - 1 - block) * TOK_DEV + half + inner).astype(jnp.int32)

def tenant_info(positions, prompt_lengths):
    lengths = prompt_lengths.astype(jnp.int32)
    starts = (jnp.cumsum(lengths) - lengths).astype(jnp.int32)
    after = starts[None, :] <= positions[:, None]
    prompt = (lax.optimization_barrier(jnp.sum(after.astype(jnp.int32), axis=1)) - 1).astype(jnp.int32)
    begin = lax.optimization_barrier(jnp.max(jnp.where(after, starts[None, :], 0), axis=1)).astype(jnp.int32)
    return (prompt, (positions - begin).astype(jnp.int32))

def reference(tokens, attn_gain, w_qkv, w_o, moe_gain, w_gate_up, w_down, expert_ids, gate_weights, prompt_lengths, page_table):
    rows = jnp.arange(TOKENS, dtype=jnp.int32)
    positions = row_positions(rows)
    prompt, relative = tenant_info(positions, prompt_lengths)
    normed = rms_scale(tokens.astype(jnp.float32), attn_gain).astype(jnp.bfloat16)
    projected = jnp.dot(normed, w_qkv.reshape(D, 3 * HEADS * HD), preferred_element_type=jnp.float32).reshape(TOKENS, 3, HEADS, HD)
    query = rotate(projected[:, 0], relative).astype(jnp.bfloat16)
    keys = rotate(projected[:, 1], relative).astype(jnp.bfloat16)
    values = projected[:, 2].astype(jnp.bfloat16)
    visible = (prompt[:, None] == prompt[None, :]) & (positions[None, :] <= positions[:, None])
    scale = HD ** (-0.5)

    def one_head(item):
        head_query, head_keys, head_values = item
        scores = jnp.dot(head_query, head_keys.T, preferred_element_type=jnp.float32) * scale
        scores = jnp.where(visible, scores, NEG)
        top = lax.optimization_barrier(jnp.max(scores, axis=1, keepdims=True))
        weights = jnp.where(visible, jnp.exp(scores - top), 0.0)
        total = lax.optimization_barrier(jnp.sum(weights, axis=1, keepdims=True))
        summed = jnp.dot(weights.astype(jnp.bfloat16), head_values, preferred_element_type=jnp.float32)
        return (summed / total).astype(jnp.bfloat16)
    heads = lax.map(one_head, (jnp.transpose(query, (1, 0, 2)), jnp.transpose(keys, (1, 0, 2)), jnp.transpose(values, (1, 0, 2))))
    heads_out = jnp.transpose(heads, (1, 0, 2)).reshape(TOKENS, HEADS * HD)
    attended = jnp.dot(heads_out, w_o, preferred_element_type=jnp.float32)
    residual = tokens.astype(jnp.float32) + attended
    moe_in = rms_scale(residual, moe_gain).astype(jnp.bfloat16)
    sources = N_BLK * N_MP
    per_dev = TOK_DEV // N_MP
    ids = expert_ids.reshape(sources, per_dev * TOP).astype(jnp.int32)
    onehot = (ids[:, :, None] == jnp.arange(EXPERTS, dtype=jnp.int32)[None, None, :]).astype(jnp.int32)
    rank = lax.optimization_barrier(jnp.sum((jnp.cumsum(onehot, axis=1) - onehot) * onehot, axis=2)).astype(jnp.int32)
    source = jnp.broadcast_to(jnp.arange(sources, dtype=jnp.int32)[:, None], ids.shape)
    token = (source * per_dev + jnp.arange(per_dev * TOP, dtype=jnp.int32)[None, :] // TOP).astype(jnp.int32)
    table = jnp.full((EXPERTS, sources * CAP), -1, jnp.int32).at[ids, source * CAP + rank].set(token)
    slice_width = FF // N_MP

    def one_expert(item):
        chosen, gate_up, down = item
        inputs = moe_in[jnp.maximum(chosen, 0)]
        both = jnp.dot(inputs, gate_up.reshape(D, 2 * FF), preferred_element_type=jnp.float32)
        hidden = (jax.nn.silu(both[:, :FF]) * both[:, FF:]).astype(jnp.bfloat16)
        total = jnp.zeros((inputs.shape[0], D), jnp.float32)
        for part in range(N_MP):
            piece = jnp.dot(hidden[:, part * slice_width:(part + 1) * slice_width], down[part * slice_width:(part + 1) * slice_width], preferred_element_type=jnp.float32)
            total = total + lax.optimization_barrier(piece.astype(jnp.bfloat16)).astype(jnp.float32)
        return total.astype(jnp.bfloat16)
    outputs = lax.map(one_expert, (table, w_gate_up, w_down)).reshape(EXPERTS * sources * CAP, D)
    index = (ids * (sources * CAP) + source * CAP + rank).reshape(TOKENS, TOP)
    picked = outputs[index]
    combined = jnp.einsum('tk,tkd->td', gate_weights.astype(jnp.float32), picked.astype(jnp.float32))
    mixed = (residual + combined).astype(jnp.bfloat16)
    pairs = jnp.stack([keys.reshape(TOKENS, HEADS * HD), values.reshape(TOKENS, HEADS * HD)], axis=1)
    page_positions = page_table.astype(jnp.int32)[:, None] * PAGE + jnp.arange(PAGE, dtype=jnp.int32)[None, :]
    cached = pairs[position_rows(page_positions)]
    kv_cache = jnp.transpose(cached, (0, 2, 1, 3))
    return (mixed, kv_cache)
```

```python
import math

import jax
import jax.numpy as jnp
from jax import lax
from jax.experimental import pallas as pl
from jax.experimental.pallas import tpu as pltpu
from jax.sharding import PartitionSpec as P

HD = 128
TOP = 6
PAGE = 128


EPS = 1e-06
THETA = 10000.0
NEG = -1e30


def rms_scale(values, gain):
    mean_sq = jnp.mean(values * values, axis=-1, keepdims=True)
    return values * lax.rsqrt(mean_sq + EPS) * gain


def rotate(values, relative):
    halfd = values.shape[-1] // 2
    inverse = THETA ** (-jnp.arange(halfd, dtype=jnp.float32) / halfd)
    angle = relative.astype(jnp.float32)[:, None] * inverse[None, :]
    cosine = jnp.cos(angle)[:, None, :]
    sine = jnp.sin(angle)[:, None, :]
    first = values[..., :halfd]
    second = values[..., halfd:]
    return jnp.concatenate(
        [first * cosine - second * sine, second * cosine + first * sine], axis=-1
    )


def row_positions(rows, tok_rows, blocks):
    half = tok_rows // 2
    device = rows // tok_rows
    inner = rows % tok_rows
    return jnp.where(
        inner < half, device * half + inner, (2 * blocks - 1 - device) * half + inner - half
    )


def tenant_info(positions, prompt_lengths):
    starts = jnp.cumsum(prompt_lengths) - prompt_lengths
    after = starts[None, :] <= positions[:, None]
    prompt = jnp.sum(after.astype(jnp.int32), axis=1) - 1
    begin = jnp.max(jnp.where(after, starts[None, :], 0), axis=1)
    return (prompt, positions - begin)


def gathered_body(
    tokens,
    attn_gain,
    w_qkv,
    w_o,
    moe_gain,
    w_gate_up,
    w_down,
    expert_ids,
    gate_weights,
    prompt_lengths,
    page_table,
):
    blocks = lax.axis_size("blk")
    shares = lax.axis_size("mp")
    block_id = lax.axis_index("blk")
    share_id = lax.axis_index("mp")
    tok_rows, width = tokens.shape
    half = tok_rows // 2
    head_cols = w_qkv.shape[2]
    local_heads = head_cols // HD
    own_rows = block_id * tok_rows + jnp.arange(tok_rows, dtype=jnp.int32)
    own_pos = row_positions(own_rows, tok_rows, blocks)
    own_prompt, relative = tenant_info(own_pos, prompt_lengths)
    normed = rms_scale(tokens.astype(jnp.float32), attn_gain).astype(jnp.bfloat16)
    projected = jnp.dot(
        normed, w_qkv.reshape(width, 3 * head_cols), preferred_element_type=jnp.float32
    ).reshape(tok_rows, 3, local_heads, HD)
    query = rotate(projected[:, 0], relative).astype(jnp.bfloat16)
    keys = rotate(projected[:, 1], relative).astype(jnp.bfloat16).reshape(tok_rows, head_cols)
    values = projected[:, 2].astype(jnp.bfloat16).reshape(tok_rows, head_cols)
    pairs = jnp.stack([keys, values], axis=1)
    query_heads = jnp.transpose(query, (1, 0, 2))
    scale = HD ** (-0.5)
    slot_count = page_table.shape[0]
    page_start = page_table * PAGE
    page_block = page_start // half
    page_inner = page_start % half
    page_row = jnp.where(
        page_block < blocks,
        page_block * tok_rows + page_inner,
        (2 * blocks - 1 - page_block) * tok_rows + half + page_inner,
    )

    def attend_block(state, piece_block, visible):
        run_max, run_sum, run_acc = state
        keys_block = piece_block[:, 0].reshape(-1, local_heads, HD)
        values_block = piece_block[:, 1].reshape(-1, local_heads, HD)
        scores = (
            jnp.einsum("hqd,khd->hqk", query_heads, keys_block, preferred_element_type=jnp.float32)
            * scale
        )
        scores = jnp.where(visible[None], scores, NEG)
        new_max = jnp.maximum(run_max, jnp.max(scores, axis=2))
        weights = jnp.where(visible[None], jnp.exp(scores - new_max[:, :, None]), 0.0)
        factor = jnp.exp(run_max - new_max)
        new_sum = run_sum * factor + jnp.sum(weights, axis=2)
        new_acc = run_acc * factor[:, :, None] + jnp.einsum(
            "hqk,khd->hqd",
            weights.astype(jnp.bfloat16),
            values_block,
            preferred_element_type=jnp.float32,
        )
        return (new_max, new_sum, new_acc)

    piece = lax.all_gather(pairs, "blk", axis=0, tiled=True)
    start = jnp.int32(0)
    run_max = jnp.full((local_heads, tok_rows), NEG, jnp.float32)
    run_sum = jnp.zeros((local_heads, tok_rows), jnp.float32)
    run_acc = jnp.zeros((local_heads, tok_rows, HD), jnp.float32)
    cache = jnp.zeros((slot_count, PAGE, 2, head_cols), jnp.bfloat16)
    count = piece.shape[0]
    step = math.gcd(count, 1024)

    def one_step(index, state):
        begin = index * step
        piece_block = lax.dynamic_slice_in_dim(piece, begin, step, 0)
        key_rows = begin + jnp.arange(step, dtype=jnp.int32)
        key_pos = row_positions(key_rows, tok_rows, blocks)
        key_prompt, key_shift = tenant_info(key_pos, prompt_lengths)
        visible = (own_prompt[:, None] == key_prompt[None, :]) & (
            key_pos[None, :] <= own_pos[:, None]
        )
        return attend_block(state, piece_block, visible)

    run_max, run_sum, run_acc = lax.fori_loop(
        0, count // step, one_step, (run_max, run_sum, run_acc)
    )
    inside = (page_row >= start) & (page_row + PAGE <= start + count)
    offset = jnp.clip(page_row, 0, count - PAGE)

    def take_page(first):
        return lax.dynamic_slice_in_dim(piece, first, PAGE, 0)

    found = jax.vmap(take_page)(offset)
    cache = jnp.where(inside[:, None, None, None], found, cache)
    run_max, run_sum, run_acc, cache = (run_max, run_sum, run_acc, cache)
    heads_out = jnp.transpose(
        (run_acc / run_sum[:, :, None]).astype(jnp.bfloat16), (1, 0, 2)
    ).reshape(tok_rows, head_cols)
    kv_cache = jnp.transpose(cache, (0, 2, 1, 3))
    partial_value = jnp.dot(heads_out, w_o, preferred_element_type=jnp.float32)
    attended = lax.psum_scatter(
        partial_value.astype(jnp.bfloat16), "mp", scatter_dimension=0, tiled=True
    ).astype(jnp.float32)
    per_dev = tok_rows // shares
    mine = lax.dynamic_slice_in_dim(tokens, share_id * per_dev, per_dev, 0)
    residual = mine.astype(jnp.float32) + attended
    moe_in = rms_scale(residual, moe_gain).astype(jnp.bfloat16)
    local_experts = w_gate_up.shape[0]
    experts = local_experts * blocks
    cap_slots = 5 * per_dev * TOP // (3 * experts)
    total_cols = experts * cap_slots
    flat_ids = expert_ids.reshape(-1)
    onehot = (flat_ids[:, None] == jnp.arange(experts, dtype=jnp.int32)[None, :]).astype(jnp.int32)
    rank = jnp.sum((jnp.cumsum(onehot, axis=0) - onehot) * onehot, axis=1)
    column = (
        flat_ids % local_experts * (blocks * cap_slots)
        + flat_ids // local_experts * cap_slots
        + rank
    )
    select = (
        (column[:, None] == jnp.arange(total_cols, dtype=jnp.int32)[None, :])
        .astype(jnp.float32)
        .reshape(per_dev, TOP, total_cols)
    )
    spread = jnp.sum(select, axis=1).astype(jnp.bfloat16)
    mixing = jnp.einsum("rk,rkc->rc", gate_weights.astype(jnp.float32), select).astype(jnp.bfloat16)
    outgoing = lax.dot_general(
        spread, moe_in, (((0,), (0,)), ((), ())), preferred_element_type=jnp.float32
    ).astype(jnp.bfloat16)
    outgoing = outgoing.reshape(local_experts, blocks, cap_slots, width)
    gate_up = w_gate_up.reshape(local_experts, width, -1)
    ff_local = w_down.shape[1]
    copies = jnp.broadcast_to(
        outgoing[:, :, None], (local_experts, blocks, shares, cap_slots, width)
    ).reshape(local_experts, blocks * shares, cap_slots, width)
    arrived = lax.all_to_all(copies, ("blk", "mp"), split_axis=1, concat_axis=1, tiled=True)
    both = jnp.einsum(
        "end,edf->enf",
        arrived.reshape(local_experts, blocks * shares * cap_slots, width),
        gate_up,
        preferred_element_type=jnp.float32,
    )
    hidden = (jax.nn.silu(both[..., :ff_local]) * both[..., ff_local:]).astype(jnp.bfloat16)
    partial_out = jnp.einsum(
        "enf,efd->end", hidden, w_down, preferred_element_type=jnp.float32
    ).astype(jnp.bfloat16)
    partial_out = partial_out.reshape(local_experts, blocks * shares, cap_slots, width)
    returned = lax.all_to_all(partial_out, ("blk", "mp"), split_axis=1, concat_axis=1, tiled=True)
    expert_out = jnp.sum(
        returned.reshape(local_experts, blocks, shares, cap_slots, width).astype(jnp.float32),
        axis=2,
    ).astype(jnp.bfloat16)
    combined = jnp.dot(
        mixing, expert_out.reshape(total_cols, width), preferred_element_type=jnp.float32
    )
    mixed = (residual + combined).astype(jnp.bfloat16)
    return (mixed, kv_cache)


Q_BLOCKS = 2
K_STEP = 512
PLANE = 8


def attend_kernel(
    info, pages, q_ref, k_own, k_other, v_own, v_other, out_ref, cache_ref, k_all, v_all, top, total, acc
):
    sources, half, _ = q_ref.shape
    count = 2 * sources
    core = info[0]

    def source(block):
        return jnp.where(block < sources, block, count - 1 - block)

    def arrange(index, _):
        mine = 2 * index + core
        theirs = 2 * index + 1 - core
        at_mine = pl.ds(pl.multiple_of(mine * half, half), half)
        at_theirs = pl.ds(pl.multiple_of(theirs * half, half), half)
        k_all[at_mine] = k_own[source(mine)]
        v_all[at_mine] = v_own[source(mine)]
        k_all[at_theirs] = k_other[source(theirs)]
        v_all[at_theirs] = v_other[source(theirs)]
        return 0

    lax.fori_loop(0, sources, arrange, 0)

    def store_page(index, _):
        at_page = pl.ds(pl.multiple_of(pages[index] * PAGE, PAGE), PAGE)
        cache_ref[index, 0] = k_all[at_page]
        cache_ref[index, 1] = v_all[at_page]
        return 0

    lax.fori_loop(0, cache_ref.shape[0], store_page, 0)

    rows = Q_BLOCKS * half
    factor = HD ** (-0.5) * math.log2(math.e)
    tenants = info.shape[0] - 1

    def begin_of(position):
        begin = jnp.zeros_like(position)
        for tenant in range(1, tenants):
            start = info[1 + tenant]
            begin = jnp.where(position >= start, start, begin)
        return begin

    def one_group(group, _):
        first_block = 2 * Q_BLOCKS * group + core
        query = jnp.concatenate(
            [q_ref[source(first_block + 2 * i)] for i in range(Q_BLOCKS)], axis=0
        )
        row = lax.broadcasted_iota(jnp.int32, (rows, 1), 0)
        q_pos = first_block * half + row + row // half * half
        begin = begin_of(q_pos)
        first = first_block * half
        last = first + (2 * Q_BLOCKS - 1) * half - 1
        k_first = begin_of(first) // K_STEP
        k_end = last // K_STEP + 1
        full_from = jnp.minimum((begin_of(last) + K_STEP - 1) // K_STEP, k_end)
        full_to = jnp.maximum(full_from, (first + 1) // K_STEP)
        top[...] = jnp.full_like(top, NEG)
        total[...] = jnp.zeros_like(total)
        acc[...] = jnp.zeros_like(acc)

        def step(masked):
            def run(index, _):
                at = pl.ds(pl.multiple_of(index * K_STEP, K_STEP), K_STEP)
                scores = lax.dot_general(
                    query, k_all[at], (((1,), (1,)), ((), ())), preferred_element_type=jnp.float32
                )
                if masked:
                    k_pos = index * K_STEP + lax.broadcasted_iota(jnp.int32, (rows, K_STEP), 1)
                    scores = jnp.where((k_pos >= begin) & (k_pos <= q_pos), scores, NEG)
                old = top[...]
                new = jnp.maximum(old, jnp.max(scores, axis=1, keepdims=True))
                weights = jnp.exp2((scores - new[:, :1]) * factor)
                shrink = jnp.exp2((old - new) * factor)
                sums = weights[:, :128]
                for part in range(1, K_STEP // 128):
                    sums = sums + weights[:, part * 128 : (part + 1) * 128]
                total[...] = total[...] * shrink + sums
                acc[...] = acc[...] * shrink + jnp.dot(
                    weights.astype(jnp.bfloat16), v_all[at], preferred_element_type=jnp.float32
                )
                top[...] = new
                return 0

            return run

        lax.fori_loop(k_first, full_from, step(True), 0)
        lax.fori_loop(full_from, full_to, step(False), 0)
        lax.fori_loop(full_to, k_end, step(True), 0)
        heads = (acc[...] / jnp.sum(total[...], axis=1, keepdims=True)).astype(jnp.bfloat16)
        for i in range(Q_BLOCKS):
            out_ref[source(first_block + 2 * i)] = heads[i * half : (i + 1) * half]
        return 0

    lax.fori_loop(0, sources // Q_BLOCKS, one_group, 0)


def attend(info, pages, query, k_own, k_other, v_own, v_other):
    sources, half, _ = query.shape
    slots = pages.shape[0]
    rows = Q_BLOCKS * half
    positions = 2 * sources * half
    vmem = pl.BlockSpec(memory_space=pltpu.VMEM)
    smem = pl.BlockSpec(memory_space=pltpu.SMEM)
    return pl.pallas_call(
        attend_kernel,
        out_shape=(
            jax.ShapeDtypeStruct((sources, half, HD), jnp.bfloat16),
            jax.ShapeDtypeStruct((slots, 2, PAGE, HD), jnp.bfloat16),
        ),
        in_specs=[smem, smem] + [vmem] * 5,
        out_specs=(vmem, vmem),
        scratch_shapes=[
            pltpu.VMEM((positions, HD), jnp.bfloat16),
            pltpu.VMEM((positions, HD), jnp.bfloat16),
            pltpu.VMEM((rows, 128), jnp.float32),
            pltpu.VMEM((rows, 128), jnp.float32),
            pltpu.VMEM((rows, HD), jnp.float32),
        ],
        compiler_params=pltpu.CompilerParams(vmem_limit_bytes=32 * 2**20),
        cost_estimate=pl.CostEstimate(
            flops=2 * 10**10, bytes_accessed=10**7, transcendentals=10**7
        ),
    )(info, pages, query, k_own, k_other, v_own, v_other)


def routed_body(
    tokens,
    attn_gain,
    w_qkv,
    w_o,
    moe_gain,
    w_gate_up,
    w_down,
    expert_ids,
    gate_weights,
    prompt_lengths,
    page_table,
):
    blocks = lax.axis_size("blk")
    block_id = lax.axis_index("blk")
    rows, width = tokens.shape
    half = rows // 2
    heads = w_qkv.shape[2] // HD
    core = block_id % 2
    planes = blocks // PLANE
    plane_id = block_id // PLANE
    experts_here = w_gate_up.shape[0]
    ff = w_down.shape[1]
    plane_groups = [[z * PLANE + p for p in range(PLANE)] for z in range(planes)]
    line_groups = [[z * PLANE + p for z in range(planes)] for p in range(PLANE)]

    own_rows = block_id * rows + jnp.arange(rows, dtype=jnp.int32)
    own_pos = row_positions(own_rows, rows, blocks)
    _, relative = tenant_info(own_pos, prompt_lengths)
    normed = rms_scale(tokens.astype(jnp.float32), attn_gain).astype(jnp.bfloat16)

    def project(part):
        return jnp.dot(normed, w_qkv[:, part], preferred_element_type=jnp.float32).reshape(
            rows, heads, HD
        )

    def by_head(values):
        cut = jnp.transpose(values.reshape(2, half, heads, HD), (2, 0, 1, 3))
        cut = jnp.where(block_id % 2 == 1, cut[:, ::-1], cut)
        return lax.all_to_all(cut.reshape(blocks, half, HD), "blk", 0, 0, tiled=True)

    keys = by_head(rotate(project(1), relative).astype(jnp.bfloat16))
    values = by_head(project(2).astype(jnp.bfloat16))
    query = by_head(rotate(project(0), relative).astype(jnp.bfloat16))
    swap = [(i, i ^ 1) for i in range(blocks)]
    k_other = lax.ppermute(keys, "blk", swap)
    v_other = lax.ppermute(values, "blk", swap)
    all_pages = lax.all_gather(page_table, "blk", axis=0, tiled=False)
    slots = all_pages.shape[1]
    core_pages = jnp.where(core == 0, all_pages[:, 0::2], all_pages[:, 1::2]).reshape(-1)
    starts = jnp.cumsum(prompt_lengths) - prompt_lengths
    info = jnp.concatenate([core[None], starts]).astype(jnp.int32)
    heads_out, cache = attend(info, core_pages, query, keys, k_other, values, v_other)
    heads_out = lax.all_to_all(heads_out, "blk", 0, 0, tiled=True).reshape(heads, 2, half, HD)
    heads_out = jnp.where(block_id % 2 == 1, heads_out[:, ::-1], heads_out)
    heads_out = jnp.transpose(heads_out, (1, 2, 0, 3)).reshape(rows, heads * HD)

    attended = jnp.dot(heads_out, w_o, preferred_element_type=jnp.float32)
    residual = tokens.astype(jnp.float32) + attended
    moe_in = rms_scale(residual, moe_gain).astype(jnp.bfloat16)

    experts = experts_here * blocks
    cap = 5 * rows * TOP // (3 * experts)
    plane_experts = experts_here * PLANE
    plane_slots = plane_experts * cap
    routing = lax.all_gather(
        jnp.concatenate([expert_ids.astype(jnp.bfloat16), gate_weights], axis=1),
        "blk",
        axis=0,
        tiled=False,
        axis_index_groups=line_groups,
    )
    named = (
        routing[:, :, :TOP, None].astype(jnp.int32)
        == plane_id * plane_experts + jnp.arange(plane_experts, dtype=jnp.int32)
    )
    weight = jnp.sum(jnp.where(named, routing[:, :, TOP:, None].astype(jnp.float32), 0.0), axis=2)
    named = jnp.any(named, axis=2)
    before = jnp.tril(jnp.ones((rows, rows), jnp.bfloat16), -1)
    rank = jnp.einsum(
        "ts,zse->zte", before, named.astype(jnp.bfloat16), preferred_element_type=jnp.float32
    )
    rank = jnp.where(named, rank, -1.0).astype(jnp.bfloat16)
    slot = jnp.arange(plane_slots, dtype=jnp.int32)
    widen = (slot[None, :] // cap == jnp.arange(plane_experts, dtype=jnp.int32)[:, None]).astype(
        jnp.bfloat16
    )
    chosen = (
        jnp.einsum("zte,es->zts", rank, widen, preferred_element_type=jnp.float32)
        == (slot % cap).astype(jnp.float32)
    )
    mixing = jnp.where(
        chosen,
        jnp.einsum(
            "zte,es->zts", weight.astype(jnp.bfloat16), widen, preferred_element_type=jnp.float32
        ),
        0.0,
    ).astype(jnp.bfloat16)
    chosen = chosen.astype(jnp.bfloat16)
    gate_up = jnp.transpose(w_gate_up, (0, 2, 1, 3))

    def to_plane(shift, rows_in):
        source = (plane_id + shift) % planes
        pick = lax.dynamic_index_in_dim(chosen, source, 0, keepdims=False)
        outgoing = lax.dot_general(
            pick, rows_in, (((0,), (0,)), ((), ())), preferred_element_type=jnp.float32
        ).astype(jnp.bfloat16)
        return lax.all_to_all(
            outgoing.reshape(PLANE, experts_here, cap, width),
            "blk",
            0,
            0,
            tiled=True,
            axis_index_groups=plane_groups,
        )

    def run_experts(arrived):
        inputs = jnp.transpose(arrived, (1, 0, 2, 3)).reshape(experts_here, PLANE * cap, width)
        gate = jnp.einsum("end,edf->enf", inputs, gate_up[:, 0], preferred_element_type=jnp.float32)
        up = jnp.einsum("end,edf->enf", inputs, gate_up[:, 1], preferred_element_type=jnp.float32)
        hidden = (jax.nn.silu(gate) * up).astype(jnp.bfloat16)
        out = jnp.einsum(
            "enf,efd->end", hidden, w_down, preferred_element_type=jnp.float32
        ).astype(jnp.bfloat16)
        return jnp.transpose(out.reshape(experts_here, PLANE, cap, width), (1, 0, 2, 3))

    def from_plane(shift, out):
        source = (plane_id + shift) % planes
        returned = lax.all_to_all(
            out, "blk", 0, 0, tiled=True, axis_index_groups=plane_groups
        ).reshape(plane_slots, width)
        mix = lax.dynamic_index_in_dim(mixing, source, 0, keepdims=False)
        return jnp.dot(mix, returned, preferred_element_type=jnp.float32)

    def along_line(values, shift):
        return lax.ppermute(
            values, "blk", [(i, (i + shift * PLANE) % blocks) for i in range(blocks)]
        )

    order = [0, 1, 3, 2]
    inputs = {s: moe_in if s == 0 else along_line(moe_in, -s) for s in order}
    outs = {s: run_experts(to_plane(s, inputs[s])) for s in order}
    mixed = residual
    for s in [1, 3, 2, 0]:
        part = from_plane(s, outs[s])
        if s != 0:
            part = along_line(part.astype(jnp.bfloat16), s).astype(jnp.float32)
        mixed = mixed + part

    cache = lax.all_to_all(
        cache.reshape(blocks, slots // 2, 2, PAGE, HD), "blk", 0, 0, tiled=True
    ).reshape(heads, 2, slots // 2, 2, PAGE, HD)
    kv_cache = jnp.transpose(cache, (2, 1, 3, 4, 0, 5)).reshape(slots, 2, PAGE, heads * HD)
    return (mixed.astype(jnp.bfloat16), kv_cache)


def body(*args):
    heads = args[2].shape[2] // HD
    by_head = lax.axis_size("mp") == 1 and 2 * heads == lax.axis_size("blk")
    return routed_body(*args) if by_head else gathered_body(*args)


def solution(mesh):
    in_specs = (
        P("blk", None),
        P(),
        P(None, None, "mp"),
        P("mp", None),
        P(),
        P("blk", None, None, "mp"),
        P("blk", "mp", None),
        P(("blk", "mp"), None),
        P(("blk", "mp"), None),
        P(),
        P("blk"),
    )
    out_specs = (P(("blk", "mp"), None), P("blk", None, None, "mp"))
    return jax.shard_map(body, mesh=mesh, in_specs=in_specs, out_specs=out_specs, check_vma=False)
```

```python
import functools
import math

import jax
import jax.numpy as jnp
from jax import lax
from jax.experimental import pallas as pl
from jax.experimental.pallas import tpu as pltpu
from jax.sharding import PartitionSpec as P

HD = 128
TOP = 6
PAGE = 128


EPS = 1e-06
THETA = 10000.0
NEG = -1e30


def rms_scale(values, gain):
    mean_sq = jnp.mean(values * values, axis=-1, keepdims=True)
    return values * lax.rsqrt(mean_sq + EPS) * gain


def rotate(values, relative):
    halfd = values.shape[-1] // 2
    inverse = THETA ** (-jnp.arange(halfd, dtype=jnp.float32) / halfd)
    angle = relative.astype(jnp.float32)[:, None] * inverse[None, :]
    cosine = jnp.cos(angle)[:, None, :]
    sine = jnp.sin(angle)[:, None, :]
    first = values[..., :halfd]
    second = values[..., halfd:]
    return jnp.concatenate(
        [first * cosine - second * sine, second * cosine + first * sine], axis=-1
    )


def row_positions(rows, tok_rows, blocks):
    half = tok_rows // 2
    device = rows // tok_rows
    inner = rows % tok_rows
    return jnp.where(
        inner < half, device * half + inner, (2 * blocks - 1 - device) * half + inner - half
    )


def tenant_info(positions, prompt_lengths):
    starts = jnp.cumsum(prompt_lengths) - prompt_lengths
    after = starts[None, :] <= positions[:, None]
    prompt = jnp.sum(after.astype(jnp.int32), axis=1) - 1
    begin = jnp.max(jnp.where(after, starts[None, :], 0), axis=1)
    return (prompt, positions - begin)


def gathered_body(
    tokens,
    attn_gain,
    w_qkv,
    w_o,
    moe_gain,
    w_gate_up,
    w_down,
    expert_ids,
    gate_weights,
    prompt_lengths,
    page_table,
):
    blocks = lax.axis_size("blk")
    shares = lax.axis_size("mp")
    block_id = lax.axis_index("blk")
    share_id = lax.axis_index("mp")
    tok_rows, width = tokens.shape
    half = tok_rows // 2
    head_cols = w_qkv.shape[2]
    local_heads = head_cols // HD
    own_rows = block_id * tok_rows + jnp.arange(tok_rows, dtype=jnp.int32)
    own_pos = row_positions(own_rows, tok_rows, blocks)
    own_prompt, relative = tenant_info(own_pos, prompt_lengths)
    normed = rms_scale(tokens.astype(jnp.float32), attn_gain).astype(jnp.bfloat16)
    projected = jnp.dot(
        normed, w_qkv.reshape(width, 3 * head_cols), preferred_element_type=jnp.float32
    ).reshape(tok_rows, 3, local_heads, HD)
    query = rotate(projected[:, 0], relative).astype(jnp.bfloat16)
    keys = rotate(projected[:, 1], relative).astype(jnp.bfloat16).reshape(tok_rows, head_cols)
    values = projected[:, 2].astype(jnp.bfloat16).reshape(tok_rows, head_cols)
    pairs = jnp.stack([keys, values], axis=1)
    query_heads = jnp.transpose(query, (1, 0, 2))
    scale = HD ** (-0.5)
    slot_count = page_table.shape[0]
    page_start = page_table * PAGE
    page_block = page_start // half
    page_inner = page_start % half
    page_row = jnp.where(
        page_block < blocks,
        page_block * tok_rows + page_inner,
        (2 * blocks - 1 - page_block) * tok_rows + half + page_inner,
    )

    def attend_block(state, piece_block, visible):
        run_max, run_sum, run_acc = state
        keys_block = piece_block[:, 0].reshape(-1, local_heads, HD)
        values_block = piece_block[:, 1].reshape(-1, local_heads, HD)
        scores = (
            jnp.einsum("hqd,khd->hqk", query_heads, keys_block, preferred_element_type=jnp.float32)
            * scale
        )
        scores = jnp.where(visible[None], scores, NEG)
        new_max = jnp.maximum(run_max, jnp.max(scores, axis=2))
        weights = jnp.where(visible[None], jnp.exp(scores - new_max[:, :, None]), 0.0)
        factor = jnp.exp(run_max - new_max)
        new_sum = run_sum * factor + jnp.sum(weights, axis=2)
        new_acc = run_acc * factor[:, :, None] + jnp.einsum(
            "hqk,khd->hqd",
            weights.astype(jnp.bfloat16),
            values_block,
            preferred_element_type=jnp.float32,
        )
        return (new_max, new_sum, new_acc)

    piece = lax.all_gather(pairs, "blk", axis=0, tiled=True)
    start = jnp.int32(0)
    run_max = jnp.full((local_heads, tok_rows), NEG, jnp.float32)
    run_sum = jnp.zeros((local_heads, tok_rows), jnp.float32)
    run_acc = jnp.zeros((local_heads, tok_rows, HD), jnp.float32)
    cache = jnp.zeros((slot_count, PAGE, 2, head_cols), jnp.bfloat16)
    count = piece.shape[0]
    step = math.gcd(count, 1024)

    def one_step(index, state):
        begin = index * step
        piece_block = lax.dynamic_slice_in_dim(piece, begin, step, 0)
        key_rows = begin + jnp.arange(step, dtype=jnp.int32)
        key_pos = row_positions(key_rows, tok_rows, blocks)
        key_prompt, key_shift = tenant_info(key_pos, prompt_lengths)
        visible = (own_prompt[:, None] == key_prompt[None, :]) & (
            key_pos[None, :] <= own_pos[:, None]
        )
        return attend_block(state, piece_block, visible)

    run_max, run_sum, run_acc = lax.fori_loop(
        0, count // step, one_step, (run_max, run_sum, run_acc)
    )
    inside = (page_row >= start) & (page_row + PAGE <= start + count)
    offset = jnp.clip(page_row, 0, count - PAGE)

    def take_page(first):
        return lax.dynamic_slice_in_dim(piece, first, PAGE, 0)

    found = jax.vmap(take_page)(offset)
    cache = jnp.where(inside[:, None, None, None], found, cache)
    run_max, run_sum, run_acc, cache = (run_max, run_sum, run_acc, cache)
    heads_out = jnp.transpose(
        (run_acc / run_sum[:, :, None]).astype(jnp.bfloat16), (1, 0, 2)
    ).reshape(tok_rows, head_cols)
    kv_cache = jnp.transpose(cache, (0, 2, 1, 3))
    partial_value = jnp.dot(heads_out, w_o, preferred_element_type=jnp.float32)
    attended = lax.psum_scatter(
        partial_value.astype(jnp.bfloat16), "mp", scatter_dimension=0, tiled=True
    ).astype(jnp.float32)
    per_dev = tok_rows // shares
    mine = lax.dynamic_slice_in_dim(tokens, share_id * per_dev, per_dev, 0)
    residual = mine.astype(jnp.float32) + attended
    moe_in = rms_scale(residual, moe_gain).astype(jnp.bfloat16)
    local_experts = w_gate_up.shape[0]
    experts = local_experts * blocks
    cap_slots = 5 * per_dev * TOP // (3 * experts)
    total_cols = experts * cap_slots
    flat_ids = expert_ids.reshape(-1)
    onehot = (flat_ids[:, None] == jnp.arange(experts, dtype=jnp.int32)[None, :]).astype(jnp.int32)
    rank = jnp.sum((jnp.cumsum(onehot, axis=0) - onehot) * onehot, axis=1)
    column = (
        flat_ids % local_experts * (blocks * cap_slots)
        + flat_ids // local_experts * cap_slots
        + rank
    )
    select = (
        (column[:, None] == jnp.arange(total_cols, dtype=jnp.int32)[None, :])
        .astype(jnp.float32)
        .reshape(per_dev, TOP, total_cols)
    )
    spread = jnp.sum(select, axis=1).astype(jnp.bfloat16)
    mixing = jnp.einsum("rk,rkc->rc", gate_weights.astype(jnp.float32), select).astype(jnp.bfloat16)
    outgoing = lax.dot_general(
        spread, moe_in, (((0,), (0,)), ((), ())), preferred_element_type=jnp.float32
    ).astype(jnp.bfloat16)
    outgoing = outgoing.reshape(local_experts, blocks, cap_slots, width)
    gate_up = w_gate_up.reshape(local_experts, width, -1)
    ff_local = w_down.shape[1]
    copies = jnp.broadcast_to(
        outgoing[:, :, None], (local_experts, blocks, shares, cap_slots, width)
    ).reshape(local_experts, blocks * shares, cap_slots, width)
    arrived = lax.all_to_all(copies, ("blk", "mp"), split_axis=1, concat_axis=1, tiled=True)
    both = jnp.einsum(
        "end,edf->enf",
        arrived.reshape(local_experts, blocks * shares * cap_slots, width),
        gate_up,
        preferred_element_type=jnp.float32,
    )
    hidden = (jax.nn.silu(both[..., :ff_local]) * both[..., ff_local:]).astype(jnp.bfloat16)
    partial_out = jnp.einsum(
        "enf,efd->end", hidden, w_down, preferred_element_type=jnp.float32
    ).astype(jnp.bfloat16)
    partial_out = partial_out.reshape(local_experts, blocks * shares, cap_slots, width)
    returned = lax.all_to_all(partial_out, ("blk", "mp"), split_axis=1, concat_axis=1, tiled=True)
    expert_out = jnp.sum(
        returned.reshape(local_experts, blocks, shares, cap_slots, width).astype(jnp.float32),
        axis=2,
    ).astype(jnp.bfloat16)
    combined = jnp.dot(
        mixing, expert_out.reshape(total_cols, width), preferred_element_type=jnp.float32
    )
    mixed = (residual + combined).astype(jnp.bfloat16)
    return (mixed, kv_cache)


Q_BLOCKS = 4
K_STEP = 1024
PLANE = 8
VMEM_BYTES = 56 * 2**20


def project_kernel(turned, flip, x_ref, w_ref, cos_ref, sin_ref, out_ref):
    rows = x_ref.shape[0]
    half = rows // 2
    projected = jnp.dot(x_ref[...], w_ref[0], preferred_element_type=jnp.float32)
    for head in range(out_ref.shape[0]):
        part = projected[:, head * HD : (head + 1) * HD]
        if turned:
            part = part * cos_ref[...] + pltpu.roll(part, HD // 2, 1) * sin_ref[...]
        part = part.astype(jnp.bfloat16)
        out_ref[head, flip[0]] = part[:half]
        out_ref[head, 1 - flip[0]] = part[half:]


def project(normed, weights, part, flip, cosine, sine, turned):
    rows, width = normed.shape
    heads = weights.shape[2] // HD
    group = 4
    return pl.pallas_call(
        functools.partial(project_kernel, turned),
        grid=(heads // group,),
        in_specs=[
            pl.BlockSpec(memory_space=pltpu.SMEM),
            pl.BlockSpec((rows, width), lambda i: (0, 0)),
            pl.BlockSpec((1, width, group * HD), lambda i: (part, 0, i)),
            pl.BlockSpec((rows, HD), lambda i: (0, 0)),
            pl.BlockSpec((rows, HD), lambda i: (0, 0)),
        ],
        out_specs=pl.BlockSpec((group, 2, rows // 2, HD), lambda i: (i, 0, 0, 0)),
        out_shape=jax.ShapeDtypeStruct((heads, 2, rows // 2, HD), jnp.bfloat16),
        compiler_params=pltpu.CompilerParams(vmem_limit_bytes=32 * 2**20),
        cost_estimate=pl.CostEstimate(
            flops=2 * rows * width * heads * HD, bytes_accessed=2 * width * heads * HD, transcendentals=0
        ),
    )(flip, normed, weights, cosine, sine)


def cache_kernel(info, pages, k_own, k_other, v_own, v_other, out_ref, sems):
    sources = k_own.shape[0]
    core = info[0]

    def copy(index, ref, which):
        page = pages[index]
        held = jnp.where(page < sources, page, 2 * sources - 1 - page)
        return pltpu.make_async_copy(ref.at[held], out_ref.at[index, which], sems.at[index, which])

    def start(index, _):
        mine = (pages[index] + core) % 2 == 0

        @pl.when(mine)
        def _():
            copy(index, k_own, 0).start()
            copy(index, v_own, 1).start()

        @pl.when(jnp.logical_not(mine))
        def _():
            copy(index, k_other, 0).start()
            copy(index, v_other, 1).start()

        return 0

    def finish(index, _):
        copy(index, k_own, 0).wait()
        copy(index, v_own, 1).wait()
        return 0

    lax.fori_loop(0, out_ref.shape[0], start, 0)
    lax.fori_loop(0, out_ref.shape[0], finish, 0)


def cache_pages(info, pages, k_own, k_other, v_own, v_other):
    smem = pl.BlockSpec(memory_space=pltpu.SMEM)
    anywhere = pl.BlockSpec(memory_space=pl.ANY)
    count = pages.shape[0]
    return pl.pallas_call(
        cache_kernel,
        out_shape=jax.ShapeDtypeStruct((count, 2) + k_own.shape[1:], jnp.bfloat16),
        in_specs=[smem, smem] + [anywhere] * 4,
        out_specs=anywhere,
        scratch_shapes=[pltpu.SemaphoreType.DMA((count, 2))],
        cost_estimate=pl.CostEstimate(flops=0, bytes_accessed=4 * k_own.size * 2, transcendentals=0),
    )(info, pages, k_own, k_other, v_own, v_other)


def attend_kernel(info, q_ref, k_own, k_other, v_own, v_other, out_ref, k_all, v_all, top, total, acc):
    sources, half, _ = q_ref.shape
    count = 2 * sources
    core = info[0]
    per_step = K_STEP // half

    def source(block):
        return jnp.where(block < sources, block, count - 1 - block)

    def arrange(index, _):
        for part in range(per_step):
            block = index * per_step + part
            held = source(block)
            mine = (block + core) % 2 == 0
            k_block = jnp.where(mine, k_own[held], k_other[held])
            v_block = jnp.where(mine, v_own[held], v_other[held])
            k_all[index, part * half : (part + 1) * half] = k_block
            v_all[index, :, part * half : (part + 1) * half] = jnp.transpose(v_block)
        return 0

    lax.fori_loop(0, count // per_step, arrange, 0)

    rows = Q_BLOCKS * half
    factor = HD ** (-0.5) * math.log2(math.e)
    tenants = info.shape[0] - 1

    def begin_of(position):
        begin = jnp.zeros_like(position)
        for tenant in range(1, tenants):
            start = info[1 + tenant]
            begin = jnp.where(position >= start, start, begin)
        return begin

    def one_group(group, _):
        first_block = 2 * Q_BLOCKS * group + core
        query = jnp.concatenate(
            [q_ref[source(first_block + 2 * i)] for i in range(Q_BLOCKS)], axis=0
        )
        row = lax.broadcasted_iota(jnp.int32, (1, rows), 1)
        q_pos = first_block * half + row + row // half * half
        begin = begin_of(q_pos)
        first = first_block * half
        last = first + (2 * Q_BLOCKS - 1) * half - 1
        k_first = begin_of(first) // K_STEP
        k_end = last // K_STEP + 1
        full_from = jnp.minimum((begin_of(last) + K_STEP - 1) // K_STEP, k_end)
        full_to = jnp.maximum(full_from, (first + 1) // K_STEP)
        top[...] = jnp.full_like(top, NEG)
        total[...] = jnp.zeros_like(total)
        acc[...] = jnp.zeros_like(acc)

        def step(masked):
            def run(index, _):
                scores = lax.dot_general(
                    k_all[index], query, (((1,), (1,)), ((), ())), preferred_element_type=jnp.float32
                )
                if masked:
                    k_pos = index * K_STEP + lax.broadcasted_iota(jnp.int32, (K_STEP, rows), 0)
                    scores = jnp.where((k_pos >= begin) & (k_pos <= q_pos), scores, NEG)
                old = top[...]
                new = jnp.maximum(old, jnp.max(scores, axis=0, keepdims=True))
                weights = jnp.exp2((scores - new) * factor)
                shrink = jnp.exp2((old - new) * factor)
                total[...] = total[...] * shrink + jnp.sum(weights, axis=0, keepdims=True)
                acc[...] = acc[...] * shrink + jnp.dot(
                    v_all[index], weights.astype(jnp.bfloat16), preferred_element_type=jnp.float32
                )
                top[...] = new
                return 0

            return run

        lax.fori_loop(k_first, full_from, step(True), 0)
        lax.fori_loop(full_from, full_to, step(False), 0)
        lax.fori_loop(full_to, k_end, step(True), 0)
        heads = jnp.transpose(acc[...] / total[...]).astype(jnp.bfloat16)
        for i in range(Q_BLOCKS):
            out_ref[source(first_block + 2 * i)] = heads[i * half : (i + 1) * half]
        return 0

    lax.fori_loop(0, sources // Q_BLOCKS, one_group, 0)


def attend(info, query, k_own, k_other, v_own, v_other):
    sources, half, _ = query.shape
    rows = Q_BLOCKS * half
    steps = 2 * sources * half // K_STEP
    vmem = pl.BlockSpec(memory_space=pltpu.VMEM)
    smem = pl.BlockSpec(memory_space=pltpu.SMEM)
    return pl.pallas_call(
        attend_kernel,
        out_shape=jax.ShapeDtypeStruct((sources, half, HD), jnp.bfloat16),
        in_specs=[smem] + [vmem] * 5,
        out_specs=vmem,
        scratch_shapes=[
            pltpu.VMEM((steps, K_STEP, HD), jnp.bfloat16),
            pltpu.VMEM((steps, HD, K_STEP), jnp.bfloat16),
            pltpu.VMEM((1, rows), jnp.float32),
            pltpu.VMEM((1, rows), jnp.float32),
            pltpu.VMEM((HD, rows), jnp.float32),
        ],
        compiler_params=pltpu.CompilerParams(vmem_limit_bytes=32 * 2**20),
        cost_estimate=pl.CostEstimate(
            flops=2 * 10**10, bytes_accessed=10**7, transcendentals=10**7
        ),
    )(info, query, k_own, k_other, v_own, v_other)


def attended_kernel(flip, heads_ref, w_ref, tokens_ref, gain_ref, residual_ref, normed_ref, joined):
    step = pl.program_id(0)
    heads, _, half, _ = heads_ref.shape
    columns = w_ref.shape[1]

    @pl.when(step == 0)
    def _():
        for head in range(heads):
            at = slice(head * HD, (head + 1) * HD)
            joined[:half, at] = heads_ref[head, flip[0]]
            joined[half:, at] = heads_ref[head, 1 - flip[0]]

    at = pl.ds(pl.multiple_of(step * columns, columns), columns)
    attended = jnp.dot(joined[...], w_ref[...], preferred_element_type=jnp.float32)
    residual_ref[:, at] = tokens_ref[:, at].astype(jnp.float32) + attended

    @pl.when(step == pl.num_programs(0) - 1)
    def _():
        residual = residual_ref[...]
        normed_ref[...] = rms_scale(residual, gain_ref[...]).astype(jnp.bfloat16)


def attended_residual(flip, heads_out, w_o, tokens, gain):
    rows, width = tokens.shape
    columns = 512
    whole = lambda *shape: pl.BlockSpec(shape, lambda i: (0,) * len(shape))
    return pl.pallas_call(
        attended_kernel,
        grid=(width // columns,),
        in_specs=[
            pl.BlockSpec(memory_space=pltpu.SMEM),
            whole(*heads_out.shape),
            pl.BlockSpec((w_o.shape[0], columns), lambda i: (0, i)),
            whole(rows, width),
            whole(1, width),
        ],
        out_specs=(whole(rows, width), whole(rows, width)),
        out_shape=(
            jax.ShapeDtypeStruct((rows, width), jnp.float32),
            jax.ShapeDtypeStruct((rows, width), jnp.bfloat16),
        ),
        scratch_shapes=[pltpu.VMEM((rows, w_o.shape[0]), jnp.bfloat16)],
        compiler_params=pltpu.CompilerParams(vmem_limit_bytes=32 * 2**20),
        cost_estimate=pl.CostEstimate(
            flops=2 * rows * width * w_o.shape[0], bytes_accessed=2 * w_o.size, transcendentals=0
        ),
    )(flip, heads_out, w_o, tokens, gain[None])


def experts_kernel(x_ref, gate_up_hbm, down_hbm, out_ref, gate_up, down, hidden, gate_up_sems, down_sems):
    experts, tiles = gate_up.shape[:2]

    def gate_up_copy(expert, tile):
        return pltpu.make_async_copy(
            gate_up_hbm.at[expert, tile], gate_up.at[expert, tile], gate_up_sems.at[expert, tile]
        )

    def down_copy(expert):
        return pltpu.make_async_copy(down_hbm.at[expert], down.at[expert], down_sems.at[expert])

    for expert in range(experts):
        for tile in range(tiles):
            gate_up_copy(expert, tile).start()
        down_copy(expert).start()

    def one_expert(expert, _):
        def one_tile(tile, _):
            gate_up_copy(expert, tile).wait()
            both = jnp.dot(x_ref[expert], gate_up[expert, tile], preferred_element_type=jnp.float32)
            gate, up = both[:, :128], both[:, 128:]
            at = pl.ds(pl.multiple_of(tile * 128, 128), 128)
            hidden[:, at] = (gate / (1.0 + jnp.exp(-gate)) * up).astype(jnp.bfloat16)
            return 0

        lax.fori_loop(0, tiles, one_tile, 0)
        down_copy(expert).wait()

        def one_column(column, _):
            at = pl.ds(pl.multiple_of(column * 512, 512), 512)
            out_ref[expert, :, at] = jnp.dot(
                hidden[...], down[expert, :, at], preferred_element_type=jnp.float32
            ).astype(jnp.bfloat16)
            return 0

        lax.fori_loop(0, out_ref.shape[2] // 512, one_column, 0)
        return 0

    lax.fori_loop(0, experts, one_expert, 0)


def run_experts(inputs, gate_up, down):
    experts, rows, width = inputs.shape
    ff = down.shape[1]
    vmem = pl.BlockSpec(memory_space=pltpu.VMEM)
    anywhere = pl.BlockSpec(memory_space=pl.ANY)
    return pl.pallas_call(
        experts_kernel,
        out_shape=jax.ShapeDtypeStruct((experts, rows, width), jnp.bfloat16),
        in_specs=[vmem, anywhere, anywhere],
        out_specs=vmem,
        scratch_shapes=[
            pltpu.VMEM(gate_up.shape, jnp.bfloat16),
            pltpu.VMEM(down.shape, jnp.bfloat16),
            pltpu.VMEM((rows, ff), jnp.bfloat16),
            pltpu.SemaphoreType.DMA(gate_up.shape[:2]),
            pltpu.SemaphoreType.DMA(down.shape[:1]),
        ],
        compiler_params=pltpu.CompilerParams(vmem_limit_bytes=VMEM_BYTES),
        cost_estimate=pl.CostEstimate(
            flops=6 * experts * rows * width * ff,
            bytes_accessed=2 * (gate_up.size + down.size + 2 * inputs.size),
            transcendentals=experts * rows * ff,
        ),
    )(inputs, gate_up, down)


def routed_body(
    tokens,
    attn_gain,
    w_qkv,
    w_o,
    moe_gain,
    w_gate_up,
    w_down,
    expert_ids,
    gate_weights,
    prompt_lengths,
    page_table,
):
    blocks = lax.axis_size("blk")
    block_id = lax.axis_index("blk")
    rows, width = tokens.shape
    half = rows // 2
    heads = w_qkv.shape[2] // HD
    core = block_id % 2
    planes = blocks // PLANE
    plane_id = block_id // PLANE
    experts_here = w_gate_up.shape[0]
    ff = w_down.shape[1]
    slots = page_table.shape[0]
    plane_groups = [[z * PLANE + p for p in range(PLANE)] for z in range(planes)]

    def exchange(values, groups=None):
        return lax.all_to_all(values, "blk", 0, 0, tiled=True, axis_index_groups=groups)

    def along_line(values, shift):
        return lax.ppermute(
            values, "blk", [(i, (i + shift * PLANE) % blocks) for i in range(blocks)]
        )

    page_rows = jnp.pad(page_table.astype(jnp.bfloat16)[None], ((0, 7), (0, 128 - slots)))
    all_pages = exchange(jnp.broadcast_to(page_rows, (blocks, 8, 128)))[:, 0, :slots].astype(jnp.int32)
    routing = jnp.concatenate([expert_ids.astype(jnp.bfloat16), gate_weights], axis=1)
    routings = [routing] + [along_line(routing, -shift) for shift in range(1, planes)]

    own_rows = block_id * rows + jnp.arange(rows, dtype=jnp.int32)
    own_pos = row_positions(own_rows, rows, blocks)
    _, relative = tenant_info(own_pos, prompt_lengths)
    normed = rms_scale(tokens.astype(jnp.float32), attn_gain).astype(jnp.bfloat16)
    inverse = THETA ** (-jnp.arange(HD // 2, dtype=jnp.float32) / (HD // 2))
    angle = relative.astype(jnp.float32)[:, None] * inverse[None, :]
    cosine, sine = jnp.cos(angle), jnp.sin(angle)
    cosine = jnp.concatenate([cosine, cosine], axis=1)
    sine = jnp.concatenate([-sine, sine], axis=1)
    by_part = jnp.transpose(w_qkv, (1, 0, 2))
    flip = core[None].astype(jnp.int32)

    def by_head(part):
        cut = project(normed, by_part, part, flip, cosine, sine, part < 2)
        return exchange(cut.reshape(blocks, half, HD))

    keys, values, query = by_head(1), by_head(2), by_head(0)
    swap = [(i, i ^ 1) for i in range(blocks)]
    k_other = lax.ppermute(keys, "blk", swap)
    v_other = lax.ppermute(values, "blk", swap)
    core_pages = jnp.where(core == 0, all_pages[:, 0::2], all_pages[:, 1::2]).reshape(-1)
    starts = jnp.cumsum(prompt_lengths) - prompt_lengths
    info = jnp.concatenate([core[None], starts]).astype(jnp.int32)
    cache = cache_pages(info, core_pages, keys, k_other, values, v_other)
    cache, query = lax.optimization_barrier((cache, query))
    cache = exchange(cache.reshape(blocks, slots // 2, 2, PAGE, HD))
    heads_out = exchange(attend(info, query, keys, k_other, values, v_other))
    residual, moe_in = attended_residual(
        flip, heads_out.reshape(heads, 2, half, HD), w_o, tokens, moe_gain
    )

    experts = experts_here * blocks
    cap = 5 * rows * TOP // (3 * experts)
    plane_experts = experts_here * PLANE
    plane_slots = plane_experts * cap
    routings = jnp.stack(routings)
    named = (
        routings[:, :, :TOP, None].astype(jnp.int32)
        == plane_id * plane_experts + jnp.arange(plane_experts, dtype=jnp.int32)
    )
    weight = jnp.sum(jnp.where(named, routings[:, :, TOP:, None].astype(jnp.float32), 0.0), axis=2)
    named = jnp.any(named, axis=2)
    before = jnp.tril(jnp.ones((rows, rows), jnp.bfloat16), -1)
    rank = jnp.einsum(
        "ts,zse->zte", before, named.astype(jnp.bfloat16), preferred_element_type=jnp.float32
    )
    rank = jnp.where(named, rank, -1.0).astype(jnp.bfloat16)
    slot = jnp.arange(plane_slots, dtype=jnp.int32)
    widen = (slot[None, :] // cap == jnp.arange(plane_experts, dtype=jnp.int32)[:, None]).astype(
        jnp.bfloat16
    )
    chosen = (
        jnp.einsum("zte,es->zts", rank, widen, preferred_element_type=jnp.float32)
        == (slot % cap).astype(jnp.float32)
    )
    mixing = jnp.where(
        chosen,
        jnp.einsum(
            "zte,es->zts", weight.astype(jnp.bfloat16), widen, preferred_element_type=jnp.float32
        ),
        0.0,
    ).astype(jnp.bfloat16)
    chosen = chosen.astype(jnp.bfloat16)
    tiles = ff // 128
    gate_up = jnp.transpose(
        w_gate_up.reshape(experts_here, width, 2, tiles, 128), (0, 3, 1, 2, 4)
    ).reshape(experts_here, tiles, width, 256)

    def plane_outputs(shift, rows_in):
        outgoing = lax.dot_general(
            chosen[shift], rows_in, (((0,), (0,)), ((), ())), preferred_element_type=jnp.float32
        ).astype(jnp.bfloat16)
        arrived = exchange(outgoing.reshape(PLANE, experts_here, cap, width), plane_groups)
        inputs = jnp.transpose(arrived, (1, 0, 2, 3)).reshape(experts_here, PLANE * cap, width)
        out = run_experts(inputs, gate_up, w_down).reshape(experts_here, PLANE, cap, width)
        returned = exchange(jnp.transpose(out, (1, 0, 2, 3)), plane_groups)
        return jnp.dot(
            mixing[shift], returned.reshape(plane_slots, width), preferred_element_type=jnp.float32
        )

    passing, parts = moe_in, {}
    parts[0] = plane_outputs(0, passing)
    for shift in range(planes - 1, 0, -1):
        passing = along_line(passing, 1)
        parts[shift] = plane_outputs(shift, passing)
    total = parts[planes - 1]
    for shift in range(planes - 2, -1, -1):
        total = parts[shift] + along_line(total.astype(jnp.bfloat16), 1).astype(jnp.float32)
    mixed = (residual + total).astype(jnp.bfloat16)

    cache = cache.reshape(heads, 2, slots // 2, 2, PAGE, HD)
    kv_cache = jnp.transpose(cache, (2, 1, 3, 4, 0, 5)).reshape(slots, 2, PAGE, heads * HD)
    return (mixed, kv_cache)


def body(*args):
    heads = args[2].shape[2] // HD
    by_head = lax.axis_size("mp") == 1 and 2 * heads == lax.axis_size("blk")
    return routed_body(*args) if by_head else gathered_body(*args)


def solution(mesh):
    in_specs = (
        P("blk", None),
        P(),
        P(None, None, "mp"),
        P("mp", None),
        P(),
        P("blk", None, None, "mp"),
        P("blk", "mp", None),
        P(("blk", "mp"), None),
        P(("blk", "mp"), None),
        P(),
        P("blk"),
    )
    out_specs = (P(("blk", "mp"), None), P("blk", None, None, "mp"))
    return jax.shard_map(body, mesh=mesh, in_specs=in_specs, out_specs=out_specs, check_vma=False)
```

```python
import functools
import math

import jax
import jax.numpy as jnp
from jax import lax
from jax.experimental import pallas as pl
from jax.experimental.pallas import tpu as pltpu
from jax.sharding import PartitionSpec as P

HD = 128
TOP = 6
PAGE = 128


EPS = 1e-06
THETA = 10000.0
NEG = -1e30


def rms_scale(values, gain):
    mean_sq = jnp.mean(values * values, axis=-1, keepdims=True)
    return values * lax.rsqrt(mean_sq + EPS) * gain


def rotate(values, relative):
    halfd = values.shape[-1] // 2
    inverse = THETA ** (-jnp.arange(halfd, dtype=jnp.float32) / halfd)
    angle = relative.astype(jnp.float32)[:, None] * inverse[None, :]
    cosine = jnp.cos(angle)[:, None, :]
    sine = jnp.sin(angle)[:, None, :]
    first = values[..., :halfd]
    second = values[..., halfd:]
    return jnp.concatenate(
        [first * cosine - second * sine, second * cosine + first * sine], axis=-1
    )


def row_positions(rows, tok_rows, blocks):
    half = tok_rows // 2
    device = rows // tok_rows
    inner = rows % tok_rows
    return jnp.where(
        inner < half, device * half + inner, (2 * blocks - 1 - device) * half + inner - half
    )


def tenant_info(positions, prompt_lengths):
    starts = jnp.cumsum(prompt_lengths) - prompt_lengths
    after = starts[None, :] <= positions[:, None]
    prompt = jnp.sum(after.astype(jnp.int32), axis=1) - 1
    begin = jnp.max(jnp.where(after, starts[None, :], 0), axis=1)
    return (prompt, positions - begin)


def gathered_body(
    tokens,
    attn_gain,
    w_qkv,
    w_o,
    moe_gain,
    w_gate_up,
    w_down,
    expert_ids,
    gate_weights,
    prompt_lengths,
    page_table,
):
    blocks = lax.axis_size("blk")
    shares = lax.axis_size("mp")
    block_id = lax.axis_index("blk")
    share_id = lax.axis_index("mp")
    tok_rows, width = tokens.shape
    half = tok_rows // 2
    head_cols = w_qkv.shape[2]
    local_heads = head_cols // HD
    own_rows = block_id * tok_rows + jnp.arange(tok_rows, dtype=jnp.int32)
    own_pos = row_positions(own_rows, tok_rows, blocks)
    own_prompt, relative = tenant_info(own_pos, prompt_lengths)
    normed = rms_scale(tokens.astype(jnp.float32), attn_gain).astype(jnp.bfloat16)
    projected = jnp.dot(
        normed, w_qkv.reshape(width, 3 * head_cols), preferred_element_type=jnp.float32
    ).reshape(tok_rows, 3, local_heads, HD)
    query = rotate(projected[:, 0], relative).astype(jnp.bfloat16)
    keys = rotate(projected[:, 1], relative).astype(jnp.bfloat16).reshape(tok_rows, head_cols)
    values = projected[:, 2].astype(jnp.bfloat16).reshape(tok_rows, head_cols)
    pairs = jnp.stack([keys, values], axis=1)
    query_heads = jnp.transpose(query, (1, 0, 2))
    scale = HD ** (-0.5)
    slot_count = page_table.shape[0]
    page_start = page_table * PAGE
    page_block = page_start // half
    page_inner = page_start % half
    page_row = jnp.where(
        page_block < blocks,
        page_block * tok_rows + page_inner,
        (2 * blocks - 1 - page_block) * tok_rows + half + page_inner,
    )

    def attend_block(state, piece_block, visible):
        run_max, run_sum, run_acc = state
        keys_block = piece_block[:, 0].reshape(-1, local_heads, HD)
        values_block = piece_block[:, 1].reshape(-1, local_heads, HD)
        scores = (
            jnp.einsum("hqd,khd->hqk", query_heads, keys_block, preferred_element_type=jnp.float32)
            * scale
        )
        scores = jnp.where(visible[None], scores, NEG)
        new_max = jnp.maximum(run_max, jnp.max(scores, axis=2))
        weights = jnp.where(visible[None], jnp.exp(scores - new_max[:, :, None]), 0.0)
        factor = jnp.exp(run_max - new_max)
        new_sum = run_sum * factor + jnp.sum(weights, axis=2)
        new_acc = run_acc * factor[:, :, None] + jnp.einsum(
            "hqk,khd->hqd",
            weights.astype(jnp.bfloat16),
            values_block,
            preferred_element_type=jnp.float32,
        )
        return (new_max, new_sum, new_acc)

    piece = lax.all_gather(pairs, "blk", axis=0, tiled=True)
    start = jnp.int32(0)
    run_max = jnp.full((local_heads, tok_rows), NEG, jnp.float32)
    run_sum = jnp.zeros((local_heads, tok_rows), jnp.float32)
    run_acc = jnp.zeros((local_heads, tok_rows, HD), jnp.float32)
    cache = jnp.zeros((slot_count, PAGE, 2, head_cols), jnp.bfloat16)
    count = piece.shape[0]
    step = math.gcd(count, 1024)

    def one_step(index, state):
        begin = index * step
        piece_block = lax.dynamic_slice_in_dim(piece, begin, step, 0)
        key_rows = begin + jnp.arange(step, dtype=jnp.int32)
        key_pos = row_positions(key_rows, tok_rows, blocks)
        key_prompt, key_shift = tenant_info(key_pos, prompt_lengths)
        visible = (own_prompt[:, None] == key_prompt[None, :]) & (
            key_pos[None, :] <= own_pos[:, None]
        )
        return attend_block(state, piece_block, visible)

    run_max, run_sum, run_acc = lax.fori_loop(
        0, count // step, one_step, (run_max, run_sum, run_acc)
    )
    inside = (page_row >= start) & (page_row + PAGE <= start + count)
    offset = jnp.clip(page_row, 0, count - PAGE)

    def take_page(first):
        return lax.dynamic_slice_in_dim(piece, first, PAGE, 0)

    found = jax.vmap(take_page)(offset)
    cache = jnp.where(inside[:, None, None, None], found, cache)
    run_max, run_sum, run_acc, cache = (run_max, run_sum, run_acc, cache)
    heads_out = jnp.transpose(
        (run_acc / run_sum[:, :, None]).astype(jnp.bfloat16), (1, 0, 2)
    ).reshape(tok_rows, head_cols)
    kv_cache = jnp.transpose(cache, (0, 2, 1, 3))
    partial_value = jnp.dot(heads_out, w_o, preferred_element_type=jnp.float32)
    attended = lax.psum_scatter(
        partial_value.astype(jnp.bfloat16), "mp", scatter_dimension=0, tiled=True
    ).astype(jnp.float32)
    per_dev = tok_rows // shares
    mine = lax.dynamic_slice_in_dim(tokens, share_id * per_dev, per_dev, 0)
    residual = mine.astype(jnp.float32) + attended
    moe_in = rms_scale(residual, moe_gain).astype(jnp.bfloat16)
    local_experts = w_gate_up.shape[0]
    experts = local_experts * blocks
    cap_slots = 5 * per_dev * TOP // (3 * experts)
    total_cols = experts * cap_slots
    flat_ids = expert_ids.reshape(-1)
    onehot = (flat_ids[:, None] == jnp.arange(experts, dtype=jnp.int32)[None, :]).astype(jnp.int32)
    rank = jnp.sum((jnp.cumsum(onehot, axis=0) - onehot) * onehot, axis=1)
    column = (
        flat_ids % local_experts * (blocks * cap_slots)
        + flat_ids // local_experts * cap_slots
        + rank
    )
    select = (
        (column[:, None] == jnp.arange(total_cols, dtype=jnp.int32)[None, :])
        .astype(jnp.float32)
        .reshape(per_dev, TOP, total_cols)
    )
    spread = jnp.sum(select, axis=1).astype(jnp.bfloat16)
    mixing = jnp.einsum("rk,rkc->rc", gate_weights.astype(jnp.float32), select).astype(jnp.bfloat16)
    outgoing = lax.dot_general(
        spread, moe_in, (((0,), (0,)), ((), ())), preferred_element_type=jnp.float32
    ).astype(jnp.bfloat16)
    outgoing = outgoing.reshape(local_experts, blocks, cap_slots, width)
    gate_up = w_gate_up.reshape(local_experts, width, -1)
    ff_local = w_down.shape[1]
    copies = jnp.broadcast_to(
        outgoing[:, :, None], (local_experts, blocks, shares, cap_slots, width)
    ).reshape(local_experts, blocks * shares, cap_slots, width)
    arrived = lax.all_to_all(copies, ("blk", "mp"), split_axis=1, concat_axis=1, tiled=True)
    both = jnp.einsum(
        "end,edf->enf",
        arrived.reshape(local_experts, blocks * shares * cap_slots, width),
        gate_up,
        preferred_element_type=jnp.float32,
    )
    hidden = (jax.nn.silu(both[..., :ff_local]) * both[..., ff_local:]).astype(jnp.bfloat16)
    partial_out = jnp.einsum(
        "enf,efd->end", hidden, w_down, preferred_element_type=jnp.float32
    ).astype(jnp.bfloat16)
    partial_out = partial_out.reshape(local_experts, blocks * shares, cap_slots, width)
    returned = lax.all_to_all(partial_out, ("blk", "mp"), split_axis=1, concat_axis=1, tiled=True)
    expert_out = jnp.sum(
        returned.reshape(local_experts, blocks, shares, cap_slots, width).astype(jnp.float32),
        axis=2,
    ).astype(jnp.bfloat16)
    combined = jnp.dot(
        mixing, expert_out.reshape(total_cols, width), preferred_element_type=jnp.float32
    )
    mixed = (residual + combined).astype(jnp.bfloat16)
    return (mixed, kv_cache)


Q_BLOCKS = 4
K_STEP = 1024
PLANE = 8
VMEM_BYTES = 56 * 2**20


def after(values, *others):
    return lax.optimization_barrier((values, others))[0]


def project_kernel(turned, flip, x_ref, w_ref, cos_ref, sin_ref, out_ref):
    rows = x_ref.shape[0]
    half = rows // 2
    projected = jnp.dot(x_ref[...], w_ref[0], preferred_element_type=jnp.float32)
    for head in range(out_ref.shape[0]):
        part = projected[:, head * HD : (head + 1) * HD]
        if turned:
            part = part * cos_ref[...] + pltpu.roll(part, HD // 2, 1) * sin_ref[...]
        part = part.astype(jnp.bfloat16)
        out_ref[head, flip[0]] = part[:half]
        out_ref[head, 1 - flip[0]] = part[half:]


def project(normed, weights, part, flip, cosine, sine, turned):
    rows, width = normed.shape
    heads = weights.shape[2] // HD
    group = 4
    return pl.pallas_call(
        functools.partial(project_kernel, turned),
        grid=(heads // group,),
        in_specs=[
            pl.BlockSpec(memory_space=pltpu.SMEM),
            pl.BlockSpec((rows, width), lambda i: (0, 0)),
            pl.BlockSpec((1, width, group * HD), lambda i: (part, 0, i)),
            pl.BlockSpec((rows, HD), lambda i: (0, 0)),
            pl.BlockSpec((rows, HD), lambda i: (0, 0)),
        ],
        out_specs=pl.BlockSpec((group, 2, rows // 2, HD), lambda i: (i, 0, 0, 0)),
        out_shape=jax.ShapeDtypeStruct((heads, 2, rows // 2, HD), jnp.bfloat16),
        compiler_params=pltpu.CompilerParams(vmem_limit_bytes=32 * 2**20),
        cost_estimate=pl.CostEstimate(
            flops=2 * rows * width * heads * HD, bytes_accessed=2 * width * heads * HD, transcendentals=0
        ),
    )(flip, normed, weights, cosine, sine)


def cache_kernel(info, pages, k_own, k_other, v_own, v_other, out_ref):
    sources = k_own.shape[0]
    core = info[0]

    def one_page(index, _):
        page = pages[index]
        held = jnp.where(page < sources, page, 2 * sources - 1 - page)
        mine = (page + core) % 2 == 0

        @pl.when(mine)
        def _():
            out_ref[index, 0] = k_own[held]
            out_ref[index, 1] = v_own[held]

        @pl.when(jnp.logical_not(mine))
        def _():
            out_ref[index, 0] = k_other[held]
            out_ref[index, 1] = v_other[held]

        return 0

    lax.fori_loop(0, out_ref.shape[0], one_page, 0)


def cache_pages(info, pages, k_own, k_other, v_own, v_other):
    smem = pl.BlockSpec(memory_space=pltpu.SMEM)
    vmem = pl.BlockSpec(memory_space=pltpu.VMEM)
    count = pages.shape[0]
    return pl.pallas_call(
        cache_kernel,
        out_shape=jax.ShapeDtypeStruct((count, 2) + k_own.shape[1:], jnp.bfloat16),
        in_specs=[smem, smem] + [vmem] * 4,
        out_specs=vmem,
        compiler_params=pltpu.CompilerParams(vmem_limit_bytes=32 * 2**20),
        cost_estimate=pl.CostEstimate(flops=0, bytes_accessed=4 * k_own.size * 2, transcendentals=0),
    )(info, pages, k_own, k_other, v_own, v_other)


def attend_kernel(info, q_ref, k_own, k_other, v_own, v_other, out_ref, k_all, v_all, top, total, acc):
    sources, half, _ = q_ref.shape
    count = 2 * sources
    core = info[0]
    per_step = K_STEP // half

    def source(block):
        return jnp.where(block < sources, block, count - 1 - block)

    def arrange(index, _):
        for part in range(per_step):
            block = index * per_step + part
            held = source(block)
            mine = (block + core) % 2 == 0
            k_block = jnp.where(mine, k_own[held], k_other[held])
            v_block = jnp.where(mine, v_own[held], v_other[held])
            k_all[index, part * half : (part + 1) * half] = k_block
            v_all[index, :, part * half : (part + 1) * half] = jnp.transpose(v_block)
        return 0

    lax.fori_loop(0, count // per_step, arrange, 0)

    rows = Q_BLOCKS * half
    factor = HD ** (-0.5) * math.log2(math.e)
    tenants = info.shape[0] - 1

    def begin_of(position):
        begin = jnp.zeros_like(position)
        for tenant in range(1, tenants):
            start = info[1 + tenant]
            begin = jnp.where(position >= start, start, begin)
        return begin

    def one_group(group, _):
        first_block = 2 * Q_BLOCKS * group + core
        query = jnp.concatenate(
            [q_ref[source(first_block + 2 * i)] for i in range(Q_BLOCKS)], axis=0
        )
        row = lax.broadcasted_iota(jnp.int32, (1, rows), 1)
        q_pos = first_block * half + row + row // half * half
        begin = begin_of(q_pos)
        first = first_block * half
        last = first + (2 * Q_BLOCKS - 1) * half - 1
        k_first = begin_of(first) // K_STEP
        k_end = last // K_STEP + 1
        full_from = jnp.minimum((begin_of(last) + K_STEP - 1) // K_STEP, k_end)
        full_to = jnp.maximum(full_from, (first + 1) // K_STEP)
        top[...] = jnp.full_like(top, NEG)
        total[...] = jnp.zeros_like(total)
        acc[...] = jnp.zeros_like(acc)

        def step(masked):
            def run(index, _):
                scores = lax.dot_general(
                    k_all[index], query, (((1,), (1,)), ((), ())), preferred_element_type=jnp.float32
                )
                if masked:
                    k_pos = index * K_STEP + lax.broadcasted_iota(jnp.int32, (K_STEP, rows), 0)
                    scores = jnp.where((k_pos >= begin) & (k_pos <= q_pos), scores, NEG)
                old = top[...]
                new = jnp.maximum(old, jnp.max(scores, axis=0, keepdims=True))
                weights = jnp.exp2((scores - new) * factor)
                shrink = jnp.exp2((old - new) * factor)
                total[...] = total[...] * shrink + jnp.sum(weights, axis=0, keepdims=True)
                acc[...] = acc[...] * shrink + jnp.dot(
                    v_all[index], weights.astype(jnp.bfloat16), preferred_element_type=jnp.float32
                )
                top[...] = new
                return 0

            return run

        lax.fori_loop(k_first, full_from, step(True), 0)
        lax.fori_loop(full_from, full_to, step(False), 0)
        lax.fori_loop(full_to, k_end, step(True), 0)
        heads = jnp.transpose(acc[...] / total[...]).astype(jnp.bfloat16)
        for i in range(Q_BLOCKS):
            out_ref[source(first_block + 2 * i)] = heads[i * half : (i + 1) * half]
        return 0

    lax.fori_loop(0, sources // Q_BLOCKS, one_group, 0)


def attend(info, query, k_own, k_other, v_own, v_other):
    sources, half, _ = query.shape
    rows = Q_BLOCKS * half
    steps = 2 * sources * half // K_STEP
    vmem = pl.BlockSpec(memory_space=pltpu.VMEM)
    smem = pl.BlockSpec(memory_space=pltpu.SMEM)
    return pl.pallas_call(
        attend_kernel,
        out_shape=jax.ShapeDtypeStruct((sources, half, HD), jnp.bfloat16),
        in_specs=[smem] + [vmem] * 5,
        out_specs=vmem,
        scratch_shapes=[
            pltpu.VMEM((steps, K_STEP, HD), jnp.bfloat16),
            pltpu.VMEM((steps, HD, K_STEP), jnp.bfloat16),
            pltpu.VMEM((1, rows), jnp.float32),
            pltpu.VMEM((1, rows), jnp.float32),
            pltpu.VMEM((HD, rows), jnp.float32),
        ],
        compiler_params=pltpu.CompilerParams(vmem_limit_bytes=32 * 2**20),
        cost_estimate=pl.CostEstimate(
            flops=2 * 10**10, bytes_accessed=10**7, transcendentals=10**7
        ),
    )(info, query, k_own, k_other, v_own, v_other)


def attended_kernel(flip, heads_ref, w_ref, tokens_ref, gain_ref, residual_ref, normed_ref, joined):
    step = pl.program_id(0)
    heads, _, half, _ = heads_ref.shape
    columns = w_ref.shape[1]

    @pl.when(step == 0)
    def _():
        for head in range(heads):
            at = slice(head * HD, (head + 1) * HD)
            joined[:half, at] = heads_ref[head, flip[0]]
            joined[half:, at] = heads_ref[head, 1 - flip[0]]

    at = pl.ds(pl.multiple_of(step * columns, columns), columns)
    attended = jnp.dot(joined[...], w_ref[...], preferred_element_type=jnp.float32)
    residual_ref[:, at] = tokens_ref[:, at].astype(jnp.float32) + attended

    @pl.when(step == pl.num_programs(0) - 1)
    def _():
        residual = residual_ref[...]
        normed_ref[...] = rms_scale(residual, gain_ref[...]).astype(jnp.bfloat16)


def attended_residual(flip, heads_out, w_o, tokens, gain):
    rows, width = tokens.shape
    columns = 512
    whole = lambda *shape: pl.BlockSpec(shape, lambda i: (0,) * len(shape))
    return pl.pallas_call(
        attended_kernel,
        grid=(width // columns,),
        in_specs=[
            pl.BlockSpec(memory_space=pltpu.SMEM),
            whole(*heads_out.shape),
            pl.BlockSpec((w_o.shape[0], columns), lambda i: (0, i)),
            whole(rows, width),
            whole(1, width),
        ],
        out_specs=(whole(rows, width), whole(rows, width)),
        out_shape=(
            jax.ShapeDtypeStruct((rows, width), jnp.float32),
            jax.ShapeDtypeStruct((rows, width), jnp.bfloat16),
        ),
        scratch_shapes=[pltpu.VMEM((rows, w_o.shape[0]), jnp.bfloat16)],
        compiler_params=pltpu.CompilerParams(vmem_limit_bytes=32 * 2**20),
        cost_estimate=pl.CostEstimate(
            flops=2 * rows * width * w_o.shape[0], bytes_accessed=2 * w_o.size, transcendentals=0
        ),
    )(flip, heads_out, w_o, tokens, gain[None])


def experts_kernel(x_ref, gate_up_hbm, down_hbm, out_ref, gate_up, down, hidden, gate_up_sems, down_sems):
    experts, tiles = gate_up.shape[:2]

    def gate_up_copy(expert, tile, which):
        at = pl.ds(pl.multiple_of(tile * 128, 128), 128)
        return pltpu.make_async_copy(
            gate_up_hbm.at[expert, which, :, at],
            gate_up.at[expert, tile, :, pl.ds(which * 128, 128)],
            gate_up_sems.at[expert, tile, which],
        )

    def down_copy(expert):
        return pltpu.make_async_copy(down_hbm.at[expert], down.at[expert], down_sems.at[expert])

    for expert in range(experts):
        for tile in range(tiles):
            gate_up_copy(expert, tile, 0).start()
            gate_up_copy(expert, tile, 1).start()
        down_copy(expert).start()

    def one_expert(expert, _):
        def one_tile(tile, _):
            gate_up_copy(expert, tile, 0).wait()
            gate_up_copy(expert, tile, 1).wait()
            both = jnp.dot(x_ref[expert], gate_up[expert, tile], preferred_element_type=jnp.float32)
            gate, up = both[:, :128], both[:, 128:]
            at = pl.ds(pl.multiple_of(tile * 128, 128), 128)
            hidden[:, at] = (gate / (1.0 + jnp.exp(-gate)) * up).astype(jnp.bfloat16)
            return 0

        lax.fori_loop(0, tiles, one_tile, 0)
        down_copy(expert).wait()

        def one_column(column, _):
            at = pl.ds(pl.multiple_of(column * 512, 512), 512)
            out_ref[expert, :, at] = jnp.dot(
                hidden[...], down[expert, :, at], preferred_element_type=jnp.float32
            ).astype(jnp.bfloat16)
            return 0

        lax.fori_loop(0, out_ref.shape[2] // 512, one_column, 0)
        return 0

    lax.fori_loop(0, experts, one_expert, 0)


def run_experts(inputs, gate_up, down):
    experts, rows, width = inputs.shape
    ff = down.shape[1]
    tiles = ff // 128
    vmem = pl.BlockSpec(memory_space=pltpu.VMEM)
    anywhere = pl.BlockSpec(memory_space=pl.ANY)
    return pl.pallas_call(
        experts_kernel,
        out_shape=jax.ShapeDtypeStruct((experts, rows, width), jnp.bfloat16),
        in_specs=[vmem, anywhere, anywhere],
        out_specs=vmem,
        scratch_shapes=[
            pltpu.VMEM((experts, tiles, width, 256), jnp.bfloat16),
            pltpu.VMEM(down.shape, jnp.bfloat16),
            pltpu.VMEM((rows, ff), jnp.bfloat16),
            pltpu.SemaphoreType.DMA((experts, tiles, 2)),
            pltpu.SemaphoreType.DMA(down.shape[:1]),
        ],
        compiler_params=pltpu.CompilerParams(vmem_limit_bytes=VMEM_BYTES),
        cost_estimate=pl.CostEstimate(
            flops=6 * experts * rows * width * ff,
            bytes_accessed=2 * (gate_up.size + down.size + 2 * inputs.size),
            transcendentals=experts * rows * ff,
        ),
    )(inputs, gate_up, down)


def routed_body(
    tokens,
    attn_gain,
    w_qkv,
    w_o,
    moe_gain,
    w_gate_up,
    w_down,
    expert_ids,
    gate_weights,
    prompt_lengths,
    page_table,
):
    blocks = lax.axis_size("blk")
    block_id = lax.axis_index("blk")
    rows, width = tokens.shape
    half = rows // 2
    heads = w_qkv.shape[2] // HD
    core = block_id % 2
    planes = blocks // PLANE
    plane_id = block_id // PLANE
    experts_here = w_gate_up.shape[0]
    slots = page_table.shape[0]
    plane_groups = [[z * PLANE + p for p in range(PLANE)] for z in range(planes)]

    def exchange(values, groups=None):
        return lax.all_to_all(values, "blk", 0, 0, tiled=True, axis_index_groups=groups)

    def along_line(values, shift):
        return lax.ppermute(
            values, "blk", [(i, (i + shift * PLANE) % blocks) for i in range(blocks)]
        )

    notes = jnp.concatenate(
        [page_table.astype(jnp.bfloat16)]
        + [part.astype(jnp.bfloat16).reshape(-1) for part in (expert_ids, gate_weights)]
    )
    named_count = rows * TOP
    note_rows = -(-notes.shape[0] // 1024) * 8
    notes = jnp.pad(notes, (0, note_rows * 128 - notes.shape[0])).reshape(note_rows, 128)
    notes = exchange(jnp.broadcast_to(notes, (blocks, note_rows, 128))).reshape(blocks, -1)

    own_rows = block_id * rows + jnp.arange(rows, dtype=jnp.int32)
    own_pos = row_positions(own_rows, rows, blocks)
    _, relative = tenant_info(own_pos, prompt_lengths)
    normed = rms_scale(tokens.astype(jnp.float32), attn_gain).astype(jnp.bfloat16)
    inverse = THETA ** (-jnp.arange(HD // 2, dtype=jnp.float32) / (HD // 2))
    angle = relative.astype(jnp.float32)[:, None] * inverse[None, :]
    cosine, sine = jnp.cos(angle), jnp.sin(angle)
    cosine = jnp.concatenate([cosine, cosine], axis=1)
    sine = jnp.concatenate([-sine, sine], axis=1)
    by_part = jnp.transpose(w_qkv, (1, 0, 2))
    flip = core[None].astype(jnp.int32)

    def by_head(part):
        cut = project(normed, by_part, part, flip, cosine, sine, part < 2)
        return cut.reshape(blocks, half, HD)

    experts = experts_here * blocks
    cap = 5 * rows * TOP // (3 * experts)
    plane_experts = experts_here * PLANE
    plane_slots = plane_experts * cap
    line = (block_id + PLANE * jnp.arange(planes)) % blocks
    routing = jnp.take(notes[:, slots : slots + 2 * named_count], line, axis=0)
    ids = routing[:, :named_count].reshape(planes, rows, TOP).astype(jnp.int32)
    gates = routing[:, named_count:].reshape(planes, rows, TOP).astype(jnp.float32)
    named = (
        ids[..., None] == plane_id * plane_experts + jnp.arange(plane_experts, dtype=jnp.int32)
    )
    weight = jnp.sum(jnp.where(named, gates[..., None], 0.0), axis=2)
    named = jnp.any(named, axis=2)
    before = jnp.tril(jnp.ones((rows, rows), jnp.bfloat16), -1)
    rank = jnp.einsum(
        "ts,zse->zte", before, named.astype(jnp.bfloat16), preferred_element_type=jnp.float32
    )
    rank = jnp.where(named, rank, -1.0).astype(jnp.bfloat16)
    slot = jnp.arange(plane_slots, dtype=jnp.int32)
    widen = (slot[None, :] // cap == jnp.arange(plane_experts, dtype=jnp.int32)[:, None]).astype(
        jnp.bfloat16
    )
    chosen = (
        jnp.einsum("zte,es->zts", rank, widen, preferred_element_type=jnp.float32)
        == (slot % cap).astype(jnp.float32)
    )
    mixing = jnp.where(
        chosen,
        jnp.einsum(
            "zte,es->zts", weight.astype(jnp.bfloat16), widen, preferred_element_type=jnp.float32
        ),
        0.0,
    ).astype(jnp.bfloat16)
    chosen = chosen.astype(jnp.bfloat16)
    values, keys = exchange(by_head(2)), exchange(by_head(1))
    query = after(by_head(0), chosen, mixing)
    w_gate_up, query = lax.optimization_barrier((w_gate_up, query))
    gate_up, query = lax.optimization_barrier(
        (jnp.transpose(w_gate_up, (0, 2, 1, 3)), exchange(query))
    )
    swap = [(i, i ^ 1) for i in range(blocks)]
    k_other = lax.ppermute(keys, "blk", swap)
    v_other = lax.ppermute(values, "blk", swap)
    all_pages = notes[:, :slots].astype(jnp.int32)
    core_pages = jnp.where(core == 0, all_pages[:, 0::2], all_pages[:, 1::2]).reshape(-1)
    starts = jnp.cumsum(prompt_lengths) - prompt_lengths
    info = jnp.concatenate([core[None], starts]).astype(jnp.int32)
    cache = cache_pages(info, core_pages, keys, k_other, values, v_other)
    cache, query = lax.optimization_barrier((cache, query))
    cache = exchange(cache.reshape(blocks, slots // 2, 2, PAGE, HD))
    heads_out = attend(info, query, keys, k_other, values, v_other)
    heads_out = exchange(after(heads_out, cache))
    residual, moe_in = attended_residual(
        flip, heads_out.reshape(heads, 2, half, HD), w_o, tokens, moe_gain
    )

    def plane_outputs(shift, rows_in):
        outgoing = lax.dot_general(
            chosen[shift], rows_in, (((0,), (0,)), ((), ())), preferred_element_type=jnp.float32
        ).astype(jnp.bfloat16)
        arrived = exchange(outgoing.reshape(PLANE, experts_here, cap, width), plane_groups)
        inputs = jnp.transpose(arrived, (1, 0, 2, 3)).reshape(experts_here, PLANE * cap, width)
        out = run_experts(inputs, gate_up, w_down).reshape(experts_here, PLANE, cap, width)
        returned = exchange(jnp.transpose(out, (1, 0, 2, 3)), plane_groups)
        return jnp.dot(
            mixing[shift], returned.reshape(plane_slots, width), preferred_element_type=jnp.float32
        )

    passing, parts = moe_in, {}
    parts[0] = plane_outputs(0, passing)
    for shift in range(planes - 1, 0, -1):
        passing = along_line(passing, 1)
        parts[shift] = plane_outputs(shift, passing)
    total = parts[planes - 1]
    for shift in range(planes - 2, -1, -1):
        total = parts[shift] + along_line(total.astype(jnp.bfloat16), 1).astype(jnp.float32)
    mixed = (residual + total).astype(jnp.bfloat16)

    cache = cache.reshape(heads, 2, slots // 2, 2, PAGE, HD)
    kv_cache = jnp.transpose(cache, (2, 1, 3, 4, 0, 5)).reshape(slots, 2, PAGE, heads * HD)
    return (mixed, kv_cache)


def body(*args):
    heads = args[2].shape[2] // HD
    by_head = lax.axis_size("mp") == 1 and 2 * heads == lax.axis_size("blk")
    return routed_body(*args) if by_head else gathered_body(*args)


def solution(mesh):
    in_specs = (
        P("blk", None),
        P(),
        P(None, None, "mp"),
        P("mp", None),
        P(),
        P("blk", None, None, "mp"),
        P("blk", "mp", None),
        P(("blk", "mp"), None),
        P(("blk", "mp"), None),
        P(),
        P("blk"),
    )
    out_specs = (P(("blk", "mp"), None), P("blk", None, None, "mp"))
    return jax.shard_map(body, mesh=mesh, in_specs=in_specs, out_specs=out_specs, check_vma=False)
```
